32 devices in a mesh: depth: 4 (over x, core), height: 2 (over y), sample: 4 (over z).
Axes of the slice: x: 2, y: 2, z: 4, core: 2. Of those that a mesh axis runs over, the one named last changes fastest.
Arguments:
- volume: bfloat16 [4, 4, 16, 8, 512], P('sample', None, 'depth', 'height'), may hold values from -6 to 6
- kernel_one: bfloat16 [32, 108], replicated, may hold values from -0.625 to 0.625
- kernel_two: bfloat16 [64, 864], P('height'), may hold values from -0.21875 to 0.21875
- cotangent: bfloat16 [4, 64, 4, 256], P('sample', 'height', 'depth'), may hold values from -24 to 24
Outputs:
- pooled_two: bfloat16 [4, 64, 4, 256], P('sample', 'height', 'depth')
- weight_grad: float32 [64, 864], P('height')
- act_grad: bfloat16 [4, 32, 8, 4, 256], P('sample', None, 'depth', 'height')
The draws below stay inside these ranges and needn't reach their ends.
All inputs are finite; a program needn't handle non-finite values.
Results may differ from the reference program's by a relative error of at most 0.005.
Values may be sent and summed in bfloat16 or wider, within the bound.
A program may use at most 64 MiB of HBM per device.

```python
import jax
import jax.numpy as jnp
from jax import lax

C0 = 4
C1 = 32
C2 = 64
WIDTH = 512
SAMPLES = 4
DEPTH = 16
HEIGHT = 8


def level_of(rng, extent, pieces, least, largest):
    def one(dim, blocks):
        steps = jax.random.uniform(jax.random.fold_in(jax.random.fold_in(rng, 6), dim), (blocks,), jnp.float32, least / len(pieces), largest / len(pieces))
        return jnp.repeat(jnp.exp(steps), extent[dim] // blocks).reshape((-1,) + (1,) * (len(extent) - dim - 1))

    gain = one(*pieces[0])
    for cut in pieces[1:]:
        gain = gain * one(*cut)
    return gain


def normal_values(own_key, extent, width, bound, pieces=(), held_as=jnp.bfloat16):
    gain = level_of(own_key, extent, pieces, -0.22, 0.18) if pieces else 1.0
    entries = jax.random.normal(own_key, extent, jnp.float32) * width * gain
    return jnp.minimum(jnp.maximum(entries, -bound), bound).astype(held_as)


def setup_inputs(seed: int = 0) -> dict:
    keys = jax.random.split(jax.random.key(seed), 5)
    return {
        "volume": normal_values(keys[0], (SAMPLES, C0, DEPTH, HEIGHT, WIDTH), 1.0, 6.0, ((0, 4), (2, 4), (3, 2))),
        "kernel_one": normal_values(keys[1], (C1, C0 * 27), (C0 * 27) ** -0.5, 0.625),
        "kernel_two": normal_values(keys[2], (C2, C1 * 27), (C1 * 27) ** -0.5, 0.21875, ((0, 2),)),
        "cotangent": normal_values(keys[3], (SAMPLES, C2, DEPTH // 4, (HEIGHT // 4) * (WIDTH // 4)), 4.0, 24.0, ((0, 4), (1, 2), (2, 4))),
    }


LEAK_SLOPE = 0.3
CONV_DIMS = ("NCDHW", "OIDHW", "NCDHW")


def activate(values):
    return LEAK_SLOPE * values + (1.0 - LEAK_SLOPE) * jax.nn.softplus(values)


def slope_at(values):
    return LEAK_SLOPE + (1.0 - LEAK_SLOPE) * jax.nn.sigmoid(values)


def pooled(values):
    count, chans, dsize, hsize, wsize = values.shape
    blocks = values.reshape(count, chans, dsize // 2, 2, hsize // 2, 2, wsize // 2, 2)
    return blocks.mean(axis=(3, 5, 7))


def spread_up(values):
    values = jnp.repeat(jnp.repeat(jnp.repeat(values, 2, axis=2), 2, axis=3), 2, axis=4)
    return values * 0.125


def conv_same(inputs, kernel):
    return lax.conv_general_dilated(inputs, kernel, (1, 1, 1), ((1, 1), (1, 1), (1, 1)),
                                    dimension_numbers=CONV_DIMS, preferred_element_type=jnp.float32)


def one_sample(vol_one, first_kernel, second_kernel, cot_one):
    pre_one = conv_same(vol_one, first_kernel)
    level_one = pooled(activate(pre_one)).astype(jnp.bfloat16)
    pre_two = conv_same(level_one, second_kernel)
    pooled_out = pooled(activate(pre_two)).astype(jnp.bfloat16)
    delta_two = (spread_up(cot_one.astype(jnp.float32)) * slope_at(pre_two)).astype(jnp.bfloat16)
    padded = jnp.pad(level_one, ((0, 0), (0, 0), (1, 1), (1, 1), (1, 1)))
    weight_part = lax.conv_general_dilated(padded, delta_two, (1, 1, 1), "VALID",
                                           dimension_numbers=("CNDHW", "IODHW", "NCDHW"),
                                           preferred_element_type=jnp.float32)
    flipped = jnp.flip(second_kernel, axis=(2, 3, 4))
    back_grad = lax.conv_general_dilated(delta_two, flipped, (1, 1, 1), ((1, 1), (1, 1), (1, 1)),
                                         dimension_numbers=("NCDHW", "IODHW", "NCDHW"),
                                         preferred_element_type=jnp.float32)
    return pooled_out[0], weight_part, back_grad[0].astype(jnp.bfloat16)


def reference(volume, kernel_one, kernel_two, cotangent):
    first_kernel = kernel_one.reshape(C1, C0, 3, 3, 3)
    second_kernel = kernel_two.reshape(C2, C1, 3, 3, 3)

    def per_sample(items):
        vol_one, cot_one = items
        cot_grid = cot_one.reshape(1, C2, DEPTH // 4, HEIGHT // 4, WIDTH // 4)
        return one_sample(vol_one[None], first_kernel, second_kernel, cot_grid)

    pooled_all, weight_parts, act_all = lax.map(per_sample, (volume, cotangent))
    scale = 1.0 / (float(SAMPLES * (DEPTH // 2) * (HEIGHT // 2) * (WIDTH // 2)) ** 0.5)
    weight_sum = jnp.sum(weight_parts * scale, axis=0)
    weight_grad = jnp.transpose(weight_sum, (1, 0, 2, 3, 4)).reshape(C2, C1 * 27)
    pooled_two = pooled_all.reshape(SAMPLES, C2, DEPTH // 4, (HEIGHT // 4) * (WIDTH // 4))
    return pooled_two, weight_grad, act_all
```

```python
import functools

import jax
import jax.numpy as jnp
import numpy as np
from jax import lax
from jax.experimental import pallas as pl
from jax.experimental.pallas import tpu as pltpu
from jax.sharding import PartitionSpec as P

LEAK_SLOPE = 0.3
CONV_DIMS = ("NCDHW", "OIDHW", "NCDHW")


def extended(block, sides, width):
    for axis, dim in sides:
        count = lax.axis_size(axis)
        forward = [(i, i + 1) for i in range(count - 1)]
        backward = [(target, source) for source, target in forward]
        low = lax.ppermute(
            lax.slice_in_dim(block, block.shape[dim] - width, None, axis=dim), axis, forward
        )
        high = lax.ppermute(lax.slice_in_dim(block, 0, width, axis=dim), axis, backward)
        block = jnp.concatenate([low, block, high], axis=dim)
    return block


def activate(values):
    return LEAK_SLOPE * values + (1.0 - LEAK_SLOPE) * jax.nn.softplus(values)


def slope_at(values):
    return LEAK_SLOPE + (1.0 - LEAK_SLOPE) * jax.nn.sigmoid(values)


def pooled(values):
    count, chans, dsize, hsize, wsize = values.shape
    blocks = values.reshape(count, chans, dsize // 2, 2, hsize // 2, 2, wsize // 2, 2)
    return blocks.mean(axis=(3, 5, 7))


def spread_up(values):
    values = jnp.repeat(jnp.repeat(jnp.repeat(values, 2, axis=2), 2, axis=3), 2, axis=4)
    return values * 0.125


def conv_valid(inputs, kernel):
    return lax.conv_general_dilated(
        inputs,
        kernel,
        (1, 1, 1),
        "VALID",
        dimension_numbers=CONV_DIMS,
        preferred_element_type=jnp.float32,
    )


def back_conv(delta_pad, kernel):
    flipped = jnp.flip(kernel, axis=(2, 3, 4))
    return lax.conv_general_dilated(
        delta_pad,
        flipped,
        (1, 1, 1),
        "VALID",
        dimension_numbers=("NCDHW", "IODHW", "NCDHW"),
        preferred_element_type=jnp.float32,
    )


def shards(volume, kernel_one, kernel_two, cotangent):
    depth_count = lax.axis_size("depth")
    height_count = lax.axis_size("height")
    sample_count = lax.axis_size("sample")
    chans_in = volume.shape[1]
    depth_loc = volume.shape[2]
    height_loc = volume.shape[3]
    width_all = volume.shape[4]
    chans_mid = kernel_one.shape[0]
    filters = kernel_two.shape[0]
    first_kernel = kernel_one.reshape(chans_mid, chans_in, 3, 3, 3)
    second_kernel = kernel_two.reshape(filters, chans_mid, 3, 3, 3)
    padded = extended(volume, (("depth", 2), ("height", 3)), 1)
    window = jnp.pad(padded, ((0, 0), (0, 0), (0, 0), (0, 0), (1, 1)))
    level_loc = pooled(activate(conv_valid(window, first_kernel))).astype(jnp.bfloat16)
    slab_rows = lax.all_gather(level_loc, "height", axis=3, tiled=True)
    level_one = extended(slab_rows, (("depth", 2),), 1)
    level_pad = jnp.pad(level_one, ((0, 0), (0, 0), (0, 0), (1, 1), (1, 1)))
    pre_two = conv_valid(level_pad, second_kernel)
    pooled_grid = pooled(activate(pre_two)).astype(jnp.bfloat16)
    depth_two = pooled_grid.shape[2]
    pooled_two = pooled_grid.reshape(
        1, filters, depth_two, pooled_grid.shape[3] * pooled_grid.shape[4]
    )
    cot_grid = cotangent.reshape(1, filters, depth_two, pooled_grid.shape[3], pooled_grid.shape[4])
    delta_two = (spread_up(cot_grid.astype(jnp.float32)) * slope_at(pre_two)).astype(jnp.bfloat16)
    weight_part = lax.conv_general_dilated(
        level_pad,
        delta_two,
        (1, 1, 1),
        "VALID",
        dimension_numbers=("CNDHW", "IODHW", "NCDHW"),
        preferred_element_type=jnp.float32,
    )
    total_cells = (
        sample_count
        * (depth_loc // 2)
        * depth_count
        * (height_loc // 2)
        * height_count
        * (width_all // 2)
    )
    scale = 1.0 / float(total_cells) ** 0.5
    weight_term = jnp.transpose(weight_part * scale, (1, 0, 2, 3, 4)).reshape(
        filters, chans_mid * 27
    )
    weight_grad = lax.psum(weight_term, ("depth", "sample"))
    delta_ext = extended(delta_two, (("depth", 2),), 1)
    delta_pad = jnp.pad(delta_ext, ((0, 0), (0, 0), (0, 0), (1, 1), (1, 1)))
    back_part = back_conv(delta_pad, second_kernel)
    act_grad = lax.psum_scatter(back_part, "height", scatter_dimension=3, tiled=True).astype(
        jnp.bfloat16
    )
    return (pooled_two, weight_grad, act_grad)


BF16 = jnp.bfloat16
F32 = jnp.float32
MESH = pl.DeviceIdType.MESH


def constants():
    parts = np.zeros((512, 6, 128), np.float32)
    for step in range(6):
        for cell in range(128):
            w = 4 * cell - 1 + step
            if 0 <= w < 512:
                parts[w, step, cell] = 1
    order = np.zeros((4, 8, 4, 6, 4, 4), np.float32)
    for step in range(6):
        for h in range(4):
            for c in range(4):
                order[h, step, c, step, h, c] = 1
    first = np.zeros((4, 3, 3, 3, 4, 4, 8, 4), np.float32)
    second = np.zeros((32, 3, 3, 3, 3, 3, 4, 32), np.float32)
    for i in range(3):
        for j in range(3):
            for k in range(3):
                for c in range(4):
                    first[c, i, j, k, i, j, k, c] = 1
                for c in range(32):
                    second[c, i, j, k, i, j, k, c] = 1
    second = np.pad(second.reshape(864, 1152), ((0, 160), (0, 0)))
    weave = np.zeros((2, 128, 256), np.float32)
    for q in range(2):
        for cell in range(128):
            weave[q, cell, 2 * cell + q] = 1
    rows = np.zeros((32, 4, 4, 32), np.float32)
    for c in range(32):
        for place in range(4):
            rows[c, place, place, c] = 1
    shaped = (
        parts.reshape(512, 768),
        order.reshape(128, 96),
        first.reshape(108, 512),
        second,
        weave.reshape(256, 256),
        rows.reshape(128, 128),
    )
    return [jnp.asarray(item, BF16) for item in shaped]


def dot(a, b):
    return jnp.dot(a, b, preferred_element_type=F32)


def dot_nt(a, b):
    return lax.dot_general(a, b, (((1,), (1,)), ((), ())), preferred_element_type=F32)


def lane_shift(values, by):
    lanes = values.shape[1]
    lane = lax.broadcasted_iota(jnp.int32, values.shape, 1)
    if by > 0:
        return jnp.where(lane >= by, pltpu.roll(values, by, 1), 0.0)
    return jnp.where(lane < lanes + by, pltpu.roll(values, lanes + by, 1), 0.0)


def kernel(
    counts, scale,
    vol, k1, k2, cot, parts, order, first, second, weave, rows,
    pooled_out, weight_out, act_out,
    raw, k2_far, cots, grid, level, delta, amat, bmat, bmat_t, wpart, wrecv, wgath,
    vol_send, vol_recv, cot_send, cot_recv, k2_send, k2_recv, w_send, w_recv, g_send, g_recv,
):
    depth_count, sample_count = counts
    group = depth_count * sample_count
    D = lax.axis_index("depth")
    H = lax.axis_index("height")
    S = lax.axis_index("sample")
    me = D * sample_count + S

    def device(d, h, s):
        return {"depth": d, "height": h, "sample": s}

    barrier = pltpu.get_barrier_semaphore()
    for step in range(1, depth_count):
        other = lax.rem(D + step, depth_count)
        for far in range(2):
            h = H if far == 0 else 1 - H
            pl.semaphore_signal(barrier, inc=1, device_id=device(other, h, S), device_id_type=MESH)
    pl.semaphore_signal(barrier, inc=1, device_id=device(D, 1 - H, S), device_id_type=MESH)
    for d_step in range(depth_count):
        for s_step in range(1, sample_count):
            pl.semaphore_signal(
                barrier, inc=1, device_id_type=MESH,
                device_id=device(
                    lax.rem(D + d_step, depth_count), H, lax.rem(S + s_step, sample_count)
                ),
            )
    pl.semaphore_wait(barrier, 2 * depth_count - 1 + depth_count * (sample_count - 1))

    def vol_copy(step, far, owner_h):
        if step == 2:
            src, dst = vol.at[3:4], raw.at[owner_h, 0:1]
        elif step == -2:
            src, dst = vol.at[0:1], raw.at[owner_h, 13:14]
        else:
            start = 5 - 4 * step
            src, dst = vol, raw.at[owner_h, start:start + 4]
        slot = (step + 2) * 2 + far
        return pltpu.make_async_remote_copy(
            src_ref=src, dst_ref=dst, send_sem=vol_send.at[slot], recv_sem=vol_recv.at[slot],
            device_id=device(D + step, H if far == 0 else 1 - H, S), device_id_type=MESH,
        )

    def cot_copy(step, far):
        slot = (step + 1) * 2 + far
        return pltpu.make_async_remote_copy(
            src_ref=cot, dst_ref=cots.at[far, 1 - step],
            send_sem=cot_send.at[slot], recv_sem=cot_recv.at[slot],
            device_id=device(D + step, H if far == 0 else 1 - H, S), device_id_type=MESH,
        )

    k2_copy = pltpu.make_async_remote_copy(
        src_ref=k2, dst_ref=k2_far, send_sem=k2_send.at[0], recv_sem=k2_recv.at[0],
        device_id=device(D, 1 - H, S), device_id_type=MESH,
    )
    vol_kinds = [(s, f) for s in (0, 1, -1, 2, -2) for f in (1, 0) if (s, f) != (0, 0)]
    cot_kinds = [(s, f) for s in (0, 1, -1) for f in (1, 0) if (s, f) != (0, 0)]

    def goes(step):
        return jnp.logical_and(D + step >= 0, D + step < depth_count)

    def comes(step):
        return jnp.logical_and(D - step >= 0, D - step < depth_count)

    for step, far in vol_kinds:
        @pl.when(goes(step))
        def _():
            vol_copy(step, far, H).start()
    k2_copy.start()
    for step, far in cot_kinds:
        @pl.when(goes(step))
        def _():
            cot_copy(step, far).start()

    raw[H, 5:9] = vol[...]
    cots[0, 1] = cot[...]
    for step in (1, 2, -1, -2):
        low, high = {1: (1, 5), 2: (0, 1), -1: (9, 13), -2: (13, 14)}[step]

        @pl.when(jnp.logical_not(comes(step)))
        def _():
            raw[:, low:high] = jnp.zeros((2, high - low, 16, 512), BF16)
            if abs(step) == 1:
                cots[0, 1 - step] = jnp.zeros((32, 256), BF16)
                cots[1, 1 - step] = jnp.zeros((32, 256), BF16)
    grid[:, 0] = jnp.zeros((14, 32, 128), BF16)
    grid[:, 9] = jnp.zeros((14, 32, 128), BF16)
    level[:, 0] = jnp.zeros((6, 128, 128), BF16)
    level[:, 5] = jnp.zeros((6, 128, 128), BF16)
    delta[:, 0] = jnp.zeros((4, 128, 128), BF16)
    delta[:, 5] = jnp.zeros((4, 128, 128), BF16)

    base = dot(k1[...], first[...])
    for wp in range(4):
        for dp in range(2):
            for hp in range(2):
                by = dp * 128 + hp * 32 + wp * 4
                row = (wp // 2) * 256 + ((wp % 2) * 4 + dp * 2 + hp) * 32
                turned = base if by == 0 else pltpu.roll(base, by, 1)
                amat[row:row + 32, :] = turned.astype(BF16)

    def spread_kernel(values, far):
        wide = dot(values, second[0:864, :])
        bmat[far * 32:far * 32 + 32, :] = wide.astype(BF16)
        bmat[64 + far * 32:96 + far * 32, :] = pltpu.roll(wide, 32, 1).astype(BF16)

    spread_kernel(k2[...], 0)

    for step, far in vol_kinds:
        @pl.when(comes(step))
        def _():
            vol_copy(step, far, H if far == 0 else 1 - H).wait_recv()

    def split_row(r, carry):
        both = jnp.concatenate([raw[0, r], raw[1, r]], axis=0)
        cut = dot(both, parts[...]).astype(BF16)
        stacked = jnp.concatenate(
            [
                jnp.concatenate(
                    [cut[h * 16:h * 16 + 16, s * 128:s * 128 + 128] for h in range(2)], axis=1
                )
                for s in range(6)
            ],
            axis=0,
        )
        placed = dot(order[...], stacked).astype(BF16)
        for h in range(8):
            grid[r, 1 + h] = placed[(h % 4) * 32:(h % 4) * 32 + 32, (h // 4) * 128:(h // 4) * 128 + 128]
        return carry

    lax.fori_loop(0, 14, split_row, 0)

    def first_layer(ld, carry):
        here = 2 * D - 2 + ld
        inside = jnp.logical_and(here >= 0, here < 2 * depth_count)
        for pair in range(2):
            cells = jnp.concatenate(
                [
                    grid[pl.ds(2 * ld, 4), 2 * lh:2 * lh + 4].reshape(512, 128)
                    for lh in (2 * pair, 2 * pair + 1)
                ],
                axis=1,
            )
            halves = []
            for q in range(2):
                z = dot(amat[q * 256:q * 256 + 256, :], cells)
                line = jnp.maximum(z, LEAK_SLOPE * z)
                more = 1.0 + jnp.exp(-jnp.abs(z))
                total = line[0:32]
                product = more[0:32]
                for i in range(1, 8):
                    total = total + line[32 * i:32 * i + 32]
                    product = product * more[32 * i:32 * i + 32]
                value = 0.125 * (total + (1.0 - LEAK_SLOPE) * jnp.log(product))
                halves.append(jnp.where(inside, value, 0.0))
            for i in range(2):
                even = halves[0][:, i * 128:i * 128 + 128]
                odd = halves[1][:, i * 128:i * 128 + 128]
                level[ld, 1 + 2 * pair + i] = jnp.concatenate(
                    [lane_shift(odd, 1), even, odd, lane_shift(even, -1)], axis=0
                ).astype(BF16)
        return carry

    lax.fori_loop(0, 6, first_layer, 0)

    k2_copy.wait_recv()
    spread_kernel(k2_far[...], 1)
    for step, far in cot_kinds:
        @pl.when(comes(step))
        def _():
            cot_copy(step, far).wait_recv()
    for kk in range(9):
        tile = bmat[:, kk * 128:kk * 128 + 128].astype(F32)
        bmat_t[:, kk * 128:kk * 128 + 128] = tile.T.astype(BF16)

    for pair in range(2):
        pool_line = jnp.zeros((32, 128), F32)
        pool_more = jnp.ones((32, 128), F32)
        for dd in range(4):
            cells = jnp.concatenate(
                [level[dd:dd + 3, lh:lh + 3].reshape(1152, 128) for lh in (2 * pair, 2 * pair + 1)],
                axis=1,
            )
            z = dot(bmat[...], cells)
            small = jnp.exp(-jnp.abs(z))
            more = 1.0 + small
            turn = 1.0 / more
            slope = LEAK_SLOPE + (1.0 - LEAK_SLOPE) * jnp.where(z >= 0, turn, small * turn)
            if dd in (1, 2):
                line = jnp.maximum(z, LEAK_SLOPE * z)
                for wp in range(2):
                    for i in range(2):
                        box = (slice(wp * 64, wp * 64 + 32), slice(i * 128, i * 128 + 128))
                        pool_line = pool_line + line[box]
                        pool_more = pool_more * more[box]
            at = (dd + 1) // 2
            near = cots[0, at, :, pair * 128:pair * 128 + 128].astype(F32)
            away = cots[1, at, :, pair * 128:pair * 128 + 128].astype(F32)
            grad = jnp.concatenate([near, away, near, away], axis=0) * 0.125
            for i in range(2):
                delta[dd, 1 + 2 * pair + i] = (grad * slope[:, i * 128:i * 128 + 128]).astype(BF16)
        value = 0.125 * (pool_line + (1.0 - LEAK_SLOPE) * jnp.log(pool_more))
        pooled_out[:, pair * 128:pair * 128 + 128] = value.astype(BF16)

    spots = [(dd, lh) for dd in (1, 2) for lh in range(4)]
    mine = jnp.concatenate(
        [
            jnp.concatenate([delta[dd, 1 + lh, 0:32], delta[dd, 1 + lh, 64:96]], axis=0)
            for dd, lh in spots
        ],
        axis=1,
    )
    folded = []
    for kd in range(3):
        for kh in range(3):
            cells = jnp.concatenate([level[dd + kd, lh + kh] for dd, lh in spots], axis=1)
            terms = dot_nt(mine, cells)
            folded.append(terms[0:32] + pltpu.roll(terms[32:64], 96, 1))
    sums = jnp.concatenate(folded, axis=1)
    coarse = sums.astype(BF16)
    fine = (sums - coarse.astype(F32)).astype(BF16)
    ordered = dot_nt(jnp.concatenate([coarse, fine], axis=0), second[...])
    ordered = (ordered[0:32] + ordered[32:64]) * scale
    for r in range(4):
        for q in range(4):
            wpart[r * 4 + q] = ordered[r * 8:r * 8 + 8, q * 256:q * 256 + 256]

    def peer(i):
        other = lax.rem(me + i, group)
        return other, device(other // sample_count, H, lax.rem(other, sample_count))

    def w_copy(i):
        other, where = peer(i)
        return pltpu.make_async_remote_copy(
            src_ref=wpart.at[other], dst_ref=wrecv.at[i], send_sem=w_send.at[i],
            recv_sem=w_recv.at[i], device_id=where, device_id_type=MESH,
        )

    def g_copy(i):
        other, where = peer(i)
        return pltpu.make_async_remote_copy(
            src_ref=wgath.at[me], dst_ref=wgath.at[me], send_sem=g_send.at[i],
            recv_sem=g_recv.at[i], device_id=where, device_id_type=MESH,
        )

    def g_arrival(i):
        other = lax.rem(me + group - i, group)
        return pltpu.make_async_remote_copy(
            src_ref=wgath.at[other], dst_ref=wgath.at[other], send_sem=g_send.at[i],
            recv_sem=g_recv.at[i], device_id=device(D, 1 - H, S), device_id_type=MESH,
        )

    def each(call):
        def body(i, carry):
            call(i)
            return carry

        lax.fori_loop(1, group, body, 0)

    each(lambda i: w_copy(i).start())

    found = []
    for od in range(2):
        cells = jnp.concatenate(
            [
                jnp.concatenate(
                    [
                        delta[od + 2 - kd, 2 * H + oh + 2 - kh]
                        for kd in range(3)
                        for kh in range(3)
                    ],
                    axis=0,
                )
                for oh in range(2)
            ],
            axis=1,
        )
        back = dot(bmat_t[...], cells)
        for oh in range(2):
            one = back[:, oh * 128:oh * 128 + 128]
            even = one[32:64] + lane_shift(one[96:128], 1)
            odd = one[64:96] + lane_shift(one[0:32], -1)
            found.append(jnp.concatenate([even, odd], axis=1).astype(BF16))
    woven = dot(jnp.concatenate(found, axis=0), weave[...]).astype(BF16)
    act_out[...] = dot(rows[...], woven).astype(BF16)

    each(lambda i: w_copy(i).wait_recv())
    chunk = wpart[me]
    for i in range(1, group):
        chunk = chunk + wrecv[i]
    wgath[me] = chunk
    each(lambda i: g_copy(i).start())
    each(lambda i: g_arrival(i).wait_recv())
    for r in range(4):
        for q in range(3):
            weight_out[r * 8:r * 8 + 8, q * 256:q * 256 + 256] = wgath[r * 4 + q]
        weight_out[r * 8:r * 8 + 8, 768:864] = wgath[r * 4 + 3, :, 0:96]

    each(lambda i: w_copy(i).wait_send())
    each(lambda i: g_copy(i).wait_send())
    for step, far in vol_kinds:
        @pl.when(goes(step))
        def _():
            vol_copy(step, far, H).wait_send()
    k2_copy.wait_send()
    for step, far in cot_kinds:
        @pl.when(goes(step))
        def _():
            cot_copy(step, far).wait_send()


def one_kernel(volume, kernel_one, kernel_two, cotangent):
    depth_count = lax.axis_size("depth")
    sample_count = lax.axis_size("sample")
    group = depth_count * sample_count
    total_cells = sample_count * 2 * depth_count * 4 * 256
    scale = 1.0 / float(total_cells) ** 0.5
    vol = jnp.transpose(volume[0], (1, 2, 0, 3)).reshape(4, 16, 512)
    vmem = pl.BlockSpec(memory_space=pltpu.VMEM)
    dma = pltpu.SemaphoreType.DMA
    pooled_two, weight_grad, act = pl.pallas_call(
        functools.partial(kernel, (depth_count, sample_count), scale),
        out_shape=(
            jax.ShapeDtypeStruct((32, 256), BF16),
            jax.ShapeDtypeStruct((32, 864), F32),
            jax.ShapeDtypeStruct((128, 256), BF16),
        ),
        in_specs=[vmem] * 10,
        out_specs=(vmem,) * 3,
        scratch_shapes=[
            pltpu.VMEM((2, 14, 16, 512), BF16),
            pltpu.VMEM((32, 864), BF16),
            pltpu.VMEM((2, 3, 32, 256), BF16),
            pltpu.VMEM((14, 10, 32, 128), BF16),
            pltpu.VMEM((6, 6, 128, 128), BF16),
            pltpu.VMEM((4, 6, 128, 128), BF16),
            pltpu.VMEM((512, 512), BF16),
            pltpu.VMEM((128, 1152), BF16),
            pltpu.VMEM((128, 1152), BF16),
            pltpu.VMEM((group, 8, 256), F32),
            pltpu.VMEM((group, 8, 256), F32),
            pltpu.VMEM((group, 8, 256), F32),
            dma((10,)), dma((10,)), dma((6,)), dma((6,)), dma((1,)), dma((1,)),
            dma((group,)), dma((group,)), dma((group,)), dma((group,)),
        ],
        compiler_params=pltpu.CompilerParams(
            collective_id=0, has_side_effects=True, vmem_limit_bytes=40 * 1024 * 1024
        ),
    )(vol, kernel_one, kernel_two, cotangent.reshape(32, 256), *constants())
    return (
        pooled_two.reshape(1, 32, 1, 256),
        weight_grad,
        act.reshape(1, 32, 2, 2, 256),
    )


def solution(mesh):
    in_specs = (
        P("sample", None, "depth", "height", None),
        P(),
        P("height", None),
        P("sample", "height", "depth", None),
    )
    out_specs = (
        P("sample", "height", "depth", None),
        P("height", None),
        P("sample", None, "depth", "height", None),
    )
    fits = mesh.shape["height"] == 2 and mesh.shape["depth"] * mesh.shape["sample"] == 16
    body = one_kernel if fits else shards
    return jax.shard_map(body, mesh=mesh, in_specs=in_specs, out_specs=out_specs, check_vma=False)
```

```python
import functools

import jax
import jax.numpy as jnp
import numpy as np
from jax import lax
from jax.experimental import pallas as pl
from jax.experimental.pallas import tpu as pltpu
from jax.sharding import PartitionSpec as P

LEAK_SLOPE = 0.3
CONV_DIMS = ("NCDHW", "OIDHW", "NCDHW")


def extended(block, sides, width):
    for axis, dim in sides:
        count = lax.axis_size(axis)
        forward = [(i, i + 1) for i in range(count - 1)]
        backward = [(target, source) for source, target in forward]
        low = lax.ppermute(
            lax.slice_in_dim(block, block.shape[dim] - width, None, axis=dim), axis, forward
        )
        high = lax.ppermute(lax.slice_in_dim(block, 0, width, axis=dim), axis, backward)
        block = jnp.concatenate([low, block, high], axis=dim)
    return block


def activate(values):
    return LEAK_SLOPE * values + (1.0 - LEAK_SLOPE) * jax.nn.softplus(values)


def slope_at(values):
    return LEAK_SLOPE + (1.0 - LEAK_SLOPE) * jax.nn.sigmoid(values)


def pooled(values):
    count, chans, dsize, hsize, wsize = values.shape
    blocks = values.reshape(count, chans, dsize // 2, 2, hsize // 2, 2, wsize // 2, 2)
    return blocks.mean(axis=(3, 5, 7))


def spread_up(values):
    values = jnp.repeat(jnp.repeat(jnp.repeat(values, 2, axis=2), 2, axis=3), 2, axis=4)
    return values * 0.125


def conv_valid(inputs, kernel):
    return lax.conv_general_dilated(
        inputs,
        kernel,
        (1, 1, 1),
        "VALID",
        dimension_numbers=CONV_DIMS,
        preferred_element_type=jnp.float32,
    )


def back_conv(delta_pad, kernel):
    flipped = jnp.flip(kernel, axis=(2, 3, 4))
    return lax.conv_general_dilated(
        delta_pad,
        flipped,
        (1, 1, 1),
        "VALID",
        dimension_numbers=("NCDHW", "IODHW", "NCDHW"),
        preferred_element_type=jnp.float32,
    )


def shards(volume, kernel_one, kernel_two, cotangent):
    depth_count = lax.axis_size("depth")
    height_count = lax.axis_size("height")
    sample_count = lax.axis_size("sample")
    chans_in = volume.shape[1]
    depth_loc = volume.shape[2]
    height_loc = volume.shape[3]
    width_all = volume.shape[4]
    chans_mid = kernel_one.shape[0]
    filters = kernel_two.shape[0]
    first_kernel = kernel_one.reshape(chans_mid, chans_in, 3, 3, 3)
    second_kernel = kernel_two.reshape(filters, chans_mid, 3, 3, 3)
    padded = extended(volume, (("depth", 2), ("height", 3)), 1)
    window = jnp.pad(padded, ((0, 0), (0, 0), (0, 0), (0, 0), (1, 1)))
    level_loc = pooled(activate(conv_valid(window, first_kernel))).astype(jnp.bfloat16)
    slab_rows = lax.all_gather(level_loc, "height", axis=3, tiled=True)
    level_one = extended(slab_rows, (("depth", 2),), 1)
    level_pad = jnp.pad(level_one, ((0, 0), (0, 0), (0, 0), (1, 1), (1, 1)))
    pre_two = conv_valid(level_pad, second_kernel)
    pooled_grid = pooled(activate(pre_two)).astype(jnp.bfloat16)
    depth_two = pooled_grid.shape[2]
    pooled_two = pooled_grid.reshape(
        1, filters, depth_two, pooled_grid.shape[3] * pooled_grid.shape[4]
    )
    cot_grid = cotangent.reshape(1, filters, depth_two, pooled_grid.shape[3], pooled_grid.shape[4])
    delta_two = (spread_up(cot_grid.astype(jnp.float32)) * slope_at(pre_two)).astype(jnp.bfloat16)
    weight_part = lax.conv_general_dilated(
        level_pad,
        delta_two,
        (1, 1, 1),
        "VALID",
        dimension_numbers=("CNDHW", "IODHW", "NCDHW"),
        preferred_element_type=jnp.float32,
    )
    total_cells = (
        sample_count
        * (depth_loc // 2)
        * depth_count
        * (height_loc // 2)
        * height_count
        * (width_all // 2)
    )
    scale = 1.0 / float(total_cells) ** 0.5
    weight_term = jnp.transpose(weight_part * scale, (1, 0, 2, 3, 4)).reshape(
        filters, chans_mid * 27
    )
    weight_grad = lax.psum(weight_term, ("depth", "sample"))
    delta_ext = extended(delta_two, (("depth", 2),), 1)
    delta_pad = jnp.pad(delta_ext, ((0, 0), (0, 0), (0, 0), (1, 1), (1, 1)))
    back_part = back_conv(delta_pad, second_kernel)
    act_grad = lax.psum_scatter(back_part, "height", scatter_dimension=3, tiled=True).astype(
        jnp.bfloat16
    )
    return (pooled_two, weight_grad, act_grad)


BF16 = jnp.bfloat16
F32 = jnp.float32
MESH = pl.DeviceIdType.MESH


def constants():
    parts = np.zeros((512, 6, 128), np.float32)
    for step in range(6):
        for cell in range(128):
            w = 4 * cell - 1 + step
            if 0 <= w < 512:
                parts[w, step, cell] = 1
    order = np.zeros((4, 8, 4, 6, 4, 4), np.float32)
    for step in range(6):
        for h in range(4):
            for c in range(4):
                order[h, step, c, step, h, c] = 1
    first = np.zeros((4, 3, 3, 3, 4, 4, 8, 4), np.float32)
    second = np.zeros((32, 3, 3, 3, 3, 3, 4, 32), np.float32)
    for i in range(3):
        for j in range(3):
            for k in range(3):
                for c in range(4):
                    first[c, i, j, k, i, j, k, c] = 1
                for c in range(32):
                    second[c, i, j, k, i, j, k, c] = 1
    second = np.pad(second.reshape(864, 1152), ((0, 160), (0, 0)))
    weave = np.zeros((2, 128, 256), np.float32)
    for q in range(2):
        for cell in range(128):
            weave[q, cell, 2 * cell + q] = 1
    rows = np.zeros((32, 4, 4, 32), np.float32)
    for c in range(32):
        for place in range(4):
            rows[c, place, place, c] = 1
    shaped = (
        parts.reshape(512, 768),
        order.reshape(128, 96),
        first.reshape(108, 512),
        second,
        weave.reshape(256, 256),
        rows.reshape(128, 128),
    )
    return [jnp.asarray(item, BF16) for item in shaped]


def dot(a, b):
    return jnp.dot(a, b, preferred_element_type=F32)


def dot_nt(a, b):
    return lax.dot_general(a, b, (((1,), (1,)), ((), ())), preferred_element_type=F32)


def lane_shift(values, by):
    lanes = values.shape[1]
    lane = lax.broadcasted_iota(jnp.int32, values.shape, 1)
    if by > 0:
        return jnp.where(lane >= by, pltpu.roll(values, by, 1), 0.0)
    return jnp.where(lane < lanes + by, pltpu.roll(values, lanes + by, 1), 0.0)


def kernel(
    counts, scale,
    vol, k1_hbm, k2_hbm, cot_hbm, parts_hbm, order_hbm, first_hbm, second_hbm, weave_hbm, rows_hbm,
    pooled_out, weight_out, act_out,
    raw, k2_far, cots, grid, level, delta, amat, bmat, bmat_t, wpart, wrecv, wgath,
    k1, k2, parts, order, first, second, weave, rows, local,
    vol_send, vol_recv, cot_send, cot_recv, k2_send, k2_recv, w_send, w_recv, g_send, g_recv,
):
    depth_count, sample_count = counts
    group = depth_count * sample_count
    D = lax.axis_index("depth")
    H = lax.axis_index("height")
    S = lax.axis_index("sample")
    me = D * sample_count + S

    def device(d, h, s):
        return {"depth": d, "height": h, "sample": s}

    barrier = pltpu.get_barrier_semaphore()
    for step in range(1, depth_count):
        other = lax.rem(D + step, depth_count)
        for far in range(2):
            h = H if far == 0 else 1 - H
            pl.semaphore_signal(barrier, inc=1, device_id=device(other, h, S), device_id_type=MESH)
    pl.semaphore_signal(barrier, inc=1, device_id=device(D, 1 - H, S), device_id_type=MESH)
    for d_step in range(depth_count):
        for s_step in range(1, sample_count):
            pl.semaphore_signal(
                barrier, inc=1, device_id_type=MESH,
                device_id=device(
                    lax.rem(D + d_step, depth_count), H, lax.rem(S + s_step, sample_count)
                ),
            )
    loads = {
        name: pltpu.make_async_copy(src, dst, local.at[i])
        for i, (name, src, dst) in enumerate(
            [
                ("k1", k1_hbm, k1), ("first", first_hbm, first), ("k2", k2_hbm, k2),
                ("second", second_hbm, second), ("parts", parts_hbm, parts),
                ("order", order_hbm, order), ("cot", cot_hbm, cots.at[0, 1]),
                ("weave", weave_hbm, weave), ("rows", rows_hbm, rows),
            ]
        )
    }
    for load in loads.values():
        load.start()

    pl.semaphore_wait(barrier, 2 * depth_count - 1 + depth_count * (sample_count - 1))

    def vol_copy(step, far, owner_h):
        if step == 2:
            src, dst = vol.at[3:4], raw.at[owner_h, 0:1]
        elif step == -2:
            src, dst = vol.at[0:1], raw.at[owner_h, 13:14]
        else:
            start = 5 - 4 * step
            src, dst = vol, raw.at[owner_h, start:start + 4]
        slot = (step + 2) * 2 + far
        return pltpu.make_async_remote_copy(
            src_ref=src, dst_ref=dst, send_sem=vol_send.at[slot], recv_sem=vol_recv.at[slot],
            device_id=device(D + step, H if far == 0 else 1 - H, S), device_id_type=MESH,
        )

    def cot_copy(step, far):
        slot = (step + 1) * 2 + far
        return pltpu.make_async_remote_copy(
            src_ref=cot_hbm, dst_ref=cots.at[far, 1 - step],
            send_sem=cot_send.at[slot], recv_sem=cot_recv.at[slot],
            device_id=device(D + step, H if far == 0 else 1 - H, S), device_id_type=MESH,
        )

    k2_copy = pltpu.make_async_remote_copy(
        src_ref=k2_hbm, dst_ref=k2_far, send_sem=k2_send.at[0], recv_sem=k2_recv.at[0],
        device_id=device(D, 1 - H, S), device_id_type=MESH,
    )
    vol_kinds = [(s, f) for s in (0, 1, -1, 2, -2) for f in (1, 0) if (s, f) != (0, 0)]
    cot_kinds = [(s, f) for s in (0, 1, -1) for f in (1, 0) if (s, f) != (0, 0)]

    def goes(step):
        return jnp.logical_and(D + step >= 0, D + step < depth_count)

    def comes(step):
        return jnp.logical_and(D - step >= 0, D - step < depth_count)

    for step, far in vol_kinds:
        @pl.when(goes(step))
        def _():
            vol_copy(step, far, H).start()
    k2_copy.start()
    for step, far in cot_kinds:
        @pl.when(goes(step))
        def _():
            cot_copy(step, far).start()

    raw[H, 5:9] = vol[...]
    for step in (1, 2, -1, -2):
        low, high = {1: (1, 5), 2: (0, 1), -1: (9, 13), -2: (13, 14)}[step]

        @pl.when(jnp.logical_not(comes(step)))
        def _():
            raw[:, low:high] = jnp.zeros((2, high - low, 16, 512), BF16)
            if abs(step) == 1:
                cots[0, 1 - step] = jnp.zeros((32, 256), BF16)
                cots[1, 1 - step] = jnp.zeros((32, 256), BF16)
    grid[:, 0] = jnp.zeros((14, 32, 128), BF16)
    grid[:, 9] = jnp.zeros((14, 32, 128), BF16)
    level[:, 0] = jnp.zeros((6, 128, 128), BF16)
    level[:, 5] = jnp.zeros((6, 128, 128), BF16)
    delta[:, 0] = jnp.zeros((4, 128, 128), BF16)
    delta[:, 5] = jnp.zeros((4, 128, 128), BF16)

    loads["k1"].wait()
    loads["first"].wait()
    base = dot(k1[...], first[...])
    for wp in range(4):
        for dp in range(2):
            for hp in range(2):
                by = dp * 128 + hp * 32 + wp * 4
                row = (wp // 2) * 256 + ((wp % 2) * 4 + dp * 2 + hp) * 32
                turned = base if by == 0 else pltpu.roll(base, by, 1)
                amat[row:row + 32, :] = turned.astype(BF16)

    def spread_kernel(values, far):
        wide = dot(values, second[0:864, :])
        bmat[far * 64:far * 64 + 32, :] = wide.astype(BF16)
        bmat[far * 64 + 32:far * 64 + 64, :] = pltpu.roll(wide, 32, 1).astype(BF16)

    loads["k2"].wait()
    loads["second"].wait()
    spread_kernel(k2[...], 0)
    loads["parts"].wait()
    loads["order"].wait()
    loads["cot"].wait()
    loads["weave"].wait()
    loads["rows"].wait()

    def split_rows(owner_h, low, high):
        count = high - low
        cut = dot(raw[owner_h, low:high].reshape(count * 16, 512), parts[...]).astype(BF16)
        stacked = jnp.concatenate(
            [
                jnp.concatenate(
                    [cut[r * 16:r * 16 + 16, s * 128:s * 128 + 128] for s in range(6)], axis=0
                )
                for r in range(count)
            ],
            axis=1,
        )
        placed = dot(order[...], stacked).astype(BF16)
        for r in range(count):
            for h in range(4):
                grid[low + r, 1 + owner_h * 4 + h] = placed[
                    h * 32:h * 32 + 32, r * 128:r * 128 + 128
                ]

    split_rows(H, 5, 9)
    for far in (0, 1):
        for step in (0, 1, -1, 2, -2):
            if (step, far) != (0, 0):
                @pl.when(comes(step))
                def _():
                    vol_copy(step, far, H if far == 0 else 1 - H).wait_recv()
        if far == 0:
            split_rows(H, 0, 5)
            split_rows(H, 9, 14)
        else:
            split_rows(1 - H, 0, 14)

    def first_layer(ld):
        here = 2 * D - 2 + ld
        inside = jnp.logical_and(here >= 0, here < 2 * depth_count)
        for pair in range(2):
            cells = jnp.concatenate(
                [
                    grid[2 * ld:2 * ld + 4, 2 * lh:2 * lh + 4].reshape(512, 128)
                    for lh in (2 * pair, 2 * pair + 1)
                ],
                axis=1,
            )
            halves = []
            for q in range(2):
                z = dot(amat[q * 256:q * 256 + 256, :], cells)
                line = jnp.maximum(z, LEAK_SLOPE * z)
                more = 1.0 + jnp.exp(-jnp.abs(z))
                total = line[0:32]
                product = more[0:32]
                for i in range(1, 8):
                    total = total + line[32 * i:32 * i + 32]
                    product = product * more[32 * i:32 * i + 32]
                value = 0.125 * (total + (1.0 - LEAK_SLOPE) * jnp.log(product))
                halves.append(jnp.where(inside, value, 0.0))
            for i in range(2):
                even = halves[0][:, i * 128:i * 128 + 128]
                odd = halves[1][:, i * 128:i * 128 + 128]
                level[ld, 1 + 2 * pair + i] = jnp.concatenate(
                    [lane_shift(odd, 1), even, odd, lane_shift(even, -1)], axis=0
                ).astype(BF16)

    for ld in (1, 2, 3, 4):
        first_layer(ld)

    def second_layer(pair, dd, sides):
        cells = jnp.concatenate(
            [level[dd:dd + 3, lh:lh + 3].reshape(1152, 128) for lh in (2 * pair, 2 * pair + 1)],
            axis=1,
        )
        low, high = sides[0] * 64, sides[-1] * 64 + 64
        z = dot(bmat[low:high, :], cells)
        small = jnp.exp(-jnp.abs(z))
        more = 1.0 + small
        turn = 1.0 / more
        slope = LEAK_SLOPE + (1.0 - LEAK_SLOPE) * jnp.where(z >= 0, turn, small * turn)
        at = (dd + 1) // 2
        grads = []
        for side in sides:
            grads += [cots[side, at, :, pair * 128:pair * 128 + 128].astype(F32)] * 2
        grad = jnp.concatenate(grads, axis=0) * 0.125
        for i in range(2):
            delta[dd, 1 + 2 * pair + i, low:high] = (
                grad * slope[:, i * 128:i * 128 + 128]
            ).astype(BF16)
        return z, more

    for pair in range(2):
        pool_line = jnp.zeros((32, 128), F32)
        pool_more = jnp.ones((32, 128), F32)
        for dd in (1, 2):
            z, more = second_layer(pair, dd, (0,))
            line = jnp.maximum(z, LEAK_SLOPE * z)
            for wp in range(2):
                for i in range(2):
                    box = (slice(wp * 32, wp * 32 + 32), slice(i * 128, i * 128 + 128))
                    pool_line = pool_line + line[box]
                    pool_more = pool_more * more[box]
        value = 0.125 * (pool_line + (1.0 - LEAK_SLOPE) * jnp.log(pool_more))
        pooled_out[:, pair * 128:pair * 128 + 128] = value.astype(BF16)

    spots = [(dd, lh) for dd in (1, 2) for lh in range(4)]
    mine = jnp.concatenate(
        [delta[dd, 1 + lh, 0:64] for dd, lh in spots], axis=1
    )
    folded = []
    for kd in range(3):
        for kh in range(3):
            cells = jnp.concatenate([level[dd + kd, lh + kh] for dd, lh in spots], axis=1)
            terms = dot_nt(mine, cells)
            folded.append(terms[0:32] + pltpu.roll(terms[32:64], 96, 1))
    sums = jnp.concatenate(folded, axis=1)
    coarse = sums.astype(BF16)
    fine = (sums - coarse.astype(F32)).astype(BF16)
    ordered = dot_nt(jnp.concatenate([coarse, fine], axis=0), second[...])
    ordered = (ordered[0:32] + ordered[32:64]) * scale
    for r in range(4):
        for q in range(4):
            wpart[r * 4 + q] = ordered[r * 8:r * 8 + 8, q * 256:q * 256 + 256]

    def peer(i):
        other = lax.rem(me + i, group)
        return other, device(other // sample_count, H, lax.rem(other, sample_count))

    def w_copy(i):
        other, where = peer(i)
        return pltpu.make_async_remote_copy(
            src_ref=wpart.at[other], dst_ref=wrecv.at[i], send_sem=w_send.at[i],
            recv_sem=w_recv.at[i], device_id=where, device_id_type=MESH,
        )

    def g_copy(i):
        other, where = peer(i)
        return pltpu.make_async_remote_copy(
            src_ref=wgath.at[me], dst_ref=wgath.at[me], send_sem=g_send.at[i],
            recv_sem=g_recv.at[i], device_id=where, device_id_type=MESH,
        )

    def g_arrival(i):
        other = lax.rem(me + group - i, group)
        return pltpu.make_async_remote_copy(
            src_ref=wgath.at[other], dst_ref=wgath.at[other], send_sem=g_send.at[i],
            recv_sem=g_recv.at[i], device_id=device(D, 1 - H, S), device_id_type=MESH,
        )

    def each(call):
        def body(i, carry):
            call(i)
            return carry

        lax.fori_loop(1, group, body, 0)

    each(lambda i: w_copy(i).start())

    first_layer(0)
    first_layer(5)
    k2_copy.wait_recv()
    spread_kernel(k2_far[...], 1)
    for kk in range(9):
        tile = bmat[:, kk * 128:kk * 128 + 128].astype(F32)
        bmat_t[:, kk * 128:kk * 128 + 128] = tile.T.astype(BF16)
    for step, far in cot_kinds:
        @pl.when(comes(step))
        def _():
            cot_copy(step, far).wait_recv()
    for pair in range(2):
        for dd, sides in ((1, (1,)), (2, (1,)), (0, (0, 1)), (3, (0, 1))):
            second_layer(pair, dd, sides)

    each(lambda i: w_copy(i).wait_recv())
    chunk = wpart[me]
    for i in range(1, group):
        chunk = chunk + wrecv[i]
    wgath[me] = chunk
    each(lambda i: g_copy(i).start())

    found = []
    for od in range(2):
        cells = jnp.concatenate(
            [
                jnp.concatenate(
                    [
                        delta[od + 2 - kd, 2 * H + oh + 2 - kh]
                        for kd in range(3)
                        for kh in range(3)
                    ],
                    axis=0,
                )
                for oh in range(2)
            ],
            axis=1,
        )
        back = dot(bmat_t[...], cells)
        for oh in range(2):
            one = back[:, oh * 128:oh * 128 + 128]
            even = one[32:64] + lane_shift(one[96:128], 1)
            odd = one[64:96] + lane_shift(one[0:32], -1)
            found.append(jnp.concatenate([even, odd], axis=1).astype(BF16))
    woven = dot(jnp.concatenate(found, axis=0), weave[...]).astype(BF16)
    act_out[...] = dot(rows[...], woven).astype(BF16)

    each(lambda i: g_arrival(i).wait_recv())
    for r in range(4):
        for q in range(3):
            weight_out[r * 8:r * 8 + 8, q * 256:q * 256 + 256] = wgath[r * 4 + q]
        weight_out[r * 8:r * 8 + 8, 768:864] = wgath[r * 4 + 3, :, 0:96]

    each(lambda i: w_copy(i).wait_send())
    each(lambda i: g_copy(i).wait_send())
    for step, far in vol_kinds:
        @pl.when(goes(step))
        def _():
            vol_copy(step, far, H).wait_send()
    k2_copy.wait_send()
    for step, far in cot_kinds:
        @pl.when(goes(step))
        def _():
            cot_copy(step, far).wait_send()


def one_kernel(volume, kernel_one, kernel_two, cotangent):
    depth_count = lax.axis_size("depth")
    sample_count = lax.axis_size("sample")
    group = depth_count * sample_count
    total_cells = sample_count * 2 * depth_count * 4 * 256
    scale = 1.0 / float(total_cells) ** 0.5
    vol = jnp.transpose(volume[0], (1, 2, 0, 3)).reshape(4, 16, 512)
    vmem = pl.BlockSpec(memory_space=pltpu.VMEM)
    hbm = pl.BlockSpec(memory_space=pltpu.HBM)
    dma = pltpu.SemaphoreType.DMA
    pooled_two, weight_grad, act = pl.pallas_call(
        functools.partial(kernel, (depth_count, sample_count), scale),
        out_shape=(
            jax.ShapeDtypeStruct((32, 256), BF16),
            jax.ShapeDtypeStruct((32, 864), F32),
            jax.ShapeDtypeStruct((128, 256), BF16),
        ),
        in_specs=[vmem] + [hbm] * 9,
        out_specs=(vmem,) * 3,
        scratch_shapes=[
            pltpu.VMEM((2, 14, 16, 512), BF16),
            pltpu.VMEM((32, 864), BF16),
            pltpu.VMEM((2, 3, 32, 256), BF16),
            pltpu.VMEM((14, 10, 32, 128), BF16),
            pltpu.VMEM((6, 6, 128, 128), BF16),
            pltpu.VMEM((4, 6, 128, 128), BF16),
            pltpu.VMEM((512, 512), BF16),
            pltpu.VMEM((128, 1152), BF16),
            pltpu.VMEM((128, 1152), BF16),
            pltpu.VMEM((group, 8, 256), F32),
            pltpu.VMEM((group, 8, 256), F32),
            pltpu.VMEM((group, 8, 256), F32),
            pltpu.VMEM((32, 108), BF16),
            pltpu.VMEM((32, 864), BF16),
            pltpu.VMEM((512, 768), BF16),
            pltpu.VMEM((128, 96), BF16),
            pltpu.VMEM((108, 512), BF16),
            pltpu.VMEM((1024, 1152), BF16),
            pltpu.VMEM((256, 256), BF16),
            pltpu.VMEM((128, 128), BF16),
            dma((9,)),
            dma((10,)), dma((10,)), dma((6,)), dma((6,)), dma((1,)), dma((1,)),
            dma((group,)), dma((group,)), dma((group,)), dma((group,)),
        ],
        compiler_params=pltpu.CompilerParams(
            collective_id=0, has_side_effects=True, vmem_limit_bytes=62 * 1024 * 1024
        ),
    )(vol, kernel_one, kernel_two, cotangent.reshape(32, 256), *constants())
    return (
        pooled_two.reshape(1, 32, 1, 256),
        weight_grad,
        act.reshape(1, 32, 2, 2, 256),
    )


def solution(mesh):
    in_specs = (
        P("sample", None, "depth", "height", None),
        P(),
        P("height", None),
        P("sample", "height", "depth", None),
    )
    out_specs = (
        P("sample", "height", "depth", None),
        P("height", None),
        P("sample", None, "depth", "height", None),
    )
    fits = mesh.shape["height"] == 2 and mesh.shape["depth"] * mesh.shape["sample"] == 16
    body = one_kernel if fits else shards
    return jax.shard_map(body, mesh=mesh, in_specs=in_specs, out_specs=out_specs, check_vma=False)
```
